256 devices in a mesh: hx: 32 (over x, z), hy: 8 (over y, core).
Axes of the slice: x: 4, y: 4, z: 8, core: 2. Of those that a mesh axis runs over, the one named last changes fastest.
Arguments:
- fine_mult: bfloat16 [152, 131072], P(None, ('hx', 'hy')), may hold values from -6 to 6
- up_operators: bfloat16 [8, 152, 152], replicated, may hold values from -0.15625 to 0.15625
- far_operators: bfloat16 [160, 152, 152], replicated, may hold values from -0.0546875 to 0.0546875
- far_list: int32 [160, 131072], P(None, ('hx', 'hy')), may hold values from -1 to 4607, as said below
- ghost_list: int32 [256, 8, 512], P(('hx', 'hy')), may hold values from -1 to 511, as said below
- coarse_list: int32 [160, 32], replicated, may hold values from -1 to 31
Outputs:
- fine_check: float32 [152, 131072], P(None, ('hx', 'hy'))
- coarse_check: float32 [152, 32], replicated
The draws below stay inside these ranges and needn't reach their ends.
Inputs may be any that keep to these rules, and one draw needn't show every extreme that they name: `far_list`: -1 means no source; a value below 512 is a box of the target's own device; a value 512 + s * 512 + j names slot j of row s of the own device's ghost_list, and that slot is never -1. ghost_list[d, s] holds distinct box numbers local to device d XOR 2**s, followed by -1; for each s some device lists all 512 boxes. `coarse_list`: -1 means no source.
All inputs are finite; a program needn't handle non-finite values.
Results may differ from the reference program's by a relative error of at most 0.009.
Values may be sent and summed in bfloat16 or wider, within the bound.
No kernel may reach another device: no remote copies, remote signals or barrier semaphores. Data moves between devices by JAX's collectives and lax.ppermute only.
A program may use at most 128 MiB of HBM per device.

```python
import jax
import jax.numpy as jnp
from jax import lax

P_SIZE = 152
OFFSETS = 160
LEVELS = 3
B = 512
BOXES = 131072
NCOARSE = 32
SECTIONS = 8
N_HX = 32
N_HY = 8


def ghost_counts(key):
    devices = N_HX * N_HY
    key_count, key_full = jax.random.split(jax.random.fold_in(key, 17))
    counts = jax.random.randint(key_count, (devices, SECTIONS), B // 8, B + 1)
    full_owner = jax.random.randint(key_full, (SECTIONS,), 0, devices)
    counts = jnp.where(jnp.arange(devices)[:, None] == full_owner[None, :], B, counts)
    return (counts, full_owner)


def draw_far_list(key, part):
    counts, full_owner = ghost_counts(key)
    key = jax.random.fold_in(key, 5)
    subkeys = jax.random.split(key, 5)
    grid_shape = (OFFSETS, BOXES)
    present = jax.random.randint(subkeys[0], grid_shape, 0, 10) < 6
    own_box = jax.random.randint(subkeys[1], grid_shape, 0, 10) < 4
    own_slot = jax.random.randint(subkeys[2], grid_shape, 0, B)
    section_pick = jax.random.randint(subkeys[3], grid_shape, 0, SECTIONS)
    raw_slot = jax.random.randint(subkeys[4], grid_shape, 0, 1 << 20)
    owner = jnp.broadcast_to(jnp.arange(BOXES)[None, :] // B, grid_shape)
    live_count = counts[owner, section_pick]
    ghost_value = B + section_pick * B + raw_slot % live_count
    values = jnp.where(present, jnp.where(own_box, own_slot, ghost_value), -1)
    corner = (jnp.arange(OFFSETS)[:, None] == 0) & (jnp.arange(BOXES)[None, :] == full_owner[SECTIONS - 1] * B)
    values = jnp.where(corner, B * (SECTIONS + 1) - 1, values)
    return values.astype(jnp.int32)


def draw_ghost_list(key, part):
    counts, full_owner = ghost_counts(key)
    key = jax.random.fold_in(key, 3)
    devices = N_HX * N_HY
    subkeys = jax.random.split(key, devices * SECTIONS)
    orders = jax.vmap(lambda single: jax.random.permutation(single, B))(subkeys).reshape(devices, SECTIONS, B)
    live_mask = jnp.arange(B)[None, None, :] < counts[:, :, None]
    return jnp.where(live_mask, orders, -1).astype(jnp.int32)


def plant(array, key, least, high):
    place = [jax.random.randint(jax.random.fold_in(key, axis), (), 0, length) for axis, length in enumerate(array.shape)]
    main_axis = array.shape.index(max(array.shape))
    neighbour = place[:main_axis] + [(place[main_axis] + 1) % array.shape[main_axis]] + place[main_axis + 1:]
    return array.at[tuple(place)].set(least).at[tuple(neighbour)].set(high)


def levels(stream_key, dims, cuts, least, high):
    level, own = 1.0, jax.random.fold_in(stream_key, 6)
    for axis_at, parts in cuts:
        heights = jnp.exp(jax.random.uniform(jax.random.fold_in(own, axis_at), (parts,), jnp.float32, least / len(cuts), high / len(cuts)))
        level = level * jnp.repeat(heights, dims[axis_at] // parts).reshape([-1 if axis == axis_at else 1 for axis in range(len(dims))])
    return level


def bell_draw(key, dims, width, limit, cuts=(), held_as=jnp.bfloat16):
    factor_of = levels(key, dims, cuts, -0.22, 0.18) if cuts else 1.0
    entries = jax.random.normal(key, dims, jnp.float32) * width * factor_of
    return jnp.minimum(jnp.maximum(entries, -limit), limit).astype(held_as)


def setup_inputs(seed: int = 0) -> dict:
    key_list = jax.random.split(jax.random.key(seed), 7)
    return {
        "fine_mult": bell_draw(key_list[0], (P_SIZE, BOXES), 1.0, 6.0, ((1, 256),)),
        "up_operators": bell_draw(key_list[1], (8, P_SIZE, P_SIZE), (8 * P_SIZE) ** -0.5, 0.15625),
        "far_operators": bell_draw(key_list[2], (OFFSETS, P_SIZE, P_SIZE), (P_SIZE * OFFSETS // 2) ** -0.5, 0.0546875),
        "far_list": draw_far_list(jax.random.fold_in(key_list[6], 71), 0),
        "ghost_list": draw_ghost_list(jax.random.fold_in(key_list[6], 71), 0),
        "coarse_list": plant(jax.random.randint(key_list[5], (OFFSETS, NCOARSE), -1, NCOARSE), jax.random.fold_in(key_list[5], 1), -1, NCOARSE - 1).astype(jnp.int32),
    }


offset_block = 32


def translate(sources, operators, lists):
    surface = operators.shape[1]
    targets = lists.shape[1]
    groups = lists.shape[0] // offset_block
    operator_blocks = operators.reshape(groups, offset_block, surface, surface)
    list_blocks = lists.reshape(groups, offset_block, targets)

    def add_block(running, pieces):
        block_ops, block_list = pieces
        live_mask = block_list >= 0
        safe_index = jnp.where(live_mask, block_list, 0).astype(jnp.int32)
        columns = jnp.take(sources, safe_index.reshape(-1), axis=1).reshape(surface, offset_block, targets)
        columns = columns * live_mask.astype(sources.dtype)[None]
        running = running + jnp.einsum("opq,qot->pt", block_ops.astype(jnp.float32), columns.astype(jnp.float32))
        return running, None

    zero_total = jnp.zeros((surface, targets), jnp.float32)
    return lax.scan(add_block, zero_total, (operator_blocks, list_blocks))[0]


def upward(multipoles, operators):
    surface, count = multipoles.shape
    children = multipoles.reshape(surface, count // 8, 8)
    return jnp.einsum("cpq,qnc->pn", operators.astype(jnp.float32), children.astype(jnp.float32))


def reference(fine_mult, up_operators, far_operators, far_list, ghost_list, coarse_list):
    devices = N_HX * N_HY

    def device_block(device):
        far_rows = lax.dynamic_slice_in_dim(far_list, device * B, B, 1)
        wanted = ghost_list[device]
        remote = jnp.clip(far_rows - B, 0, SECTIONS * B - 1)
        section_of = remote // B
        slot_of = remote % B
        partner = jnp.bitwise_xor(device, jnp.left_shift(jnp.int32(1), section_of))
        remote_box = partner * B + wanted[section_of, slot_of]
        global_id = jnp.where(far_rows < 0, -1, jnp.where(far_rows < B, device * B + far_rows, remote_box))
        return translate(fine_mult, far_operators, global_id.astype(jnp.int32))

    blocks = lax.map(device_block, jnp.arange(devices, dtype=jnp.int32))
    fine_check = jnp.transpose(blocks, (1, 0, 2)).reshape(P_SIZE, BOXES)
    multipoles = fine_mult
    for level_step in range(LEVELS):
        multipoles = upward(multipoles, up_operators).astype(jnp.bfloat16)
    coarse = upward(multipoles, up_operators).astype(jnp.bfloat16)
    coarse_check = translate(coarse, far_operators, coarse_list)
    return fine_check, coarse_check
```

```python
import functools

import jax
import jax.numpy as jnp
from jax import lax
from jax.experimental import pallas as pl
from jax.experimental.pallas import tpu as pltpu
from jax.sharding import PartitionSpec as P

LEVELS = 3
LANES = 128
NT = (((1,), (1,)), ((), ()))


def from_partner(value, axis, stride):
    mask = 2**stride
    pairs = [(source, source ^ mask) for source in range(lax.axis_size(axis))]
    return lax.ppermute(value, axis, pairs)


def lift(rows, up_ref):
    surface = up_ref.shape[1]
    count = rows.shape[1] // 8
    total = None
    for octant in range(8):
        children = jnp.concatenate([rows[half, pl.ds(octant, count, stride=8), :] for half in range(2)], axis=1)
        children = children[:, :surface].astype(jnp.bfloat16)
        term = lax.dot_general(children, up_ref[octant], NT, preferred_element_type=jnp.float32)
        total = term if total is None else total + term
    return total


def upward_kernel(fine_ref, up_ref, out_ref, *levels):
    surface, boxes = fine_ref.shape
    spot = lax.broadcasted_iota(jnp.int32, (boxes, boxes), 0) == lax.broadcasted_iota(jnp.int32, (boxes, boxes), 1)
    rows = lax.dot_general(
        spot.astype(jnp.float32).astype(jnp.bfloat16), fine_ref[...], NT, preferred_element_type=jnp.float32
    )
    for level in levels:
        level[0] = rows[:, :LANES]
        level[1, :, : surface - LANES] = rows[:, LANES:]
        rows = lift(level, up_ref).astype(jnp.bfloat16).astype(jnp.float32)
    out_ref[...] = rows


def upward(fine_mult, up_operators):
    surface, boxes = fine_mult.shape
    return pl.pallas_call(
        upward_kernel,
        out_shape=jax.ShapeDtypeStruct((boxes // 8**LEVELS, surface), jnp.float32),
        scratch_shapes=[pltpu.VMEM((2, boxes // 8**level, LANES), jnp.float32) for level in range(LEVELS)],
        name="upward",
    )(fine_mult, up_operators)


def translate_kernel(sections, idx_hbm, slots_ref, poles_ref, up_ref, far_ref, *rest):
    blocks = rest[:sections]
    fine_out, coarse_out, table, buf_a, buf_b, acc, poles, idx_a, idx_b, sem = rest[sections:]
    step = pl.program_id(0)
    pairs = pl.num_programs(0) - 1
    surface = far_ref.shape[1]
    boxes = blocks[0].shape[1]
    targets = acc.shape[0]
    tail = surface - LANES

    def fetch(pair, where, slot):
        return [
            pltpu.make_async_copy(idx_hbm.at[2 * pair + k], where.at[k], sem.at[slot, k]) for k in range(2)
        ]

    def put(first, rows):
        count = rows.shape[0]
        table[pl.ds(2 * first, count, stride=2), :] = rows[:, :LANES]
        table[pl.ds(2 * first + 1, count, stride=2), :] = jnp.concatenate(
            [rows[:, LANES:], jnp.zeros((count, LANES - tail), jnp.float32)], axis=1
        )

    def gather(where, buf):
        for k in range(2):
            for target in range(targets):
                buf[k, 2 * target : 2 * target + 2, :] = table[pl.ds(where[k, target], 2), :]

    def multiply(buf):
        rows, weights = [], []
        for k in range(2):
            rows += [buf[k, pl.ds(0, targets, stride=2), :], buf[k, pl.ds(1, targets, stride=2), :]]
            weights += [far_ref[k], jnp.zeros((surface, LANES - tail), jnp.bfloat16)]
        rows = jnp.concatenate([piece.astype(jnp.bfloat16) for piece in rows], axis=1)
        weights = jnp.concatenate(weights, axis=1)
        acc[...] += lax.dot_general(rows, weights, NT, preferred_element_type=jnp.float32)

    @pl.when(step == 0)
    def _():
        for copy in fetch(0, idx_a, 0):
            copy.start()
        acc[...] = jnp.zeros_like(acc)
        number = lax.broadcasted_iota(jnp.int32, (boxes, boxes), 1)
        for section in range(sections):
            spot = (slots_ref[:, section : section + 1] == number).astype(jnp.float32).astype(jnp.bfloat16)
            put(
                section * boxes,
                lax.dot_general(spot, blocks[section][...], NT, preferred_element_type=jnp.float32),
            )
        poles[0] = poles_ref[:, :LANES]
        poles[1, :, :tail] = poles_ref[:, LANES:]
        coarse = lift(poles, up_ref).astype(jnp.bfloat16).astype(jnp.float32)
        put(sections * boxes, coarse)
        put(sections * boxes + coarse.shape[0], jnp.zeros((8, surface), jnp.float32))

    even = step % 2 == 0

    @pl.when(jnp.logical_and(even, step < pairs))
    def _():
        for copy in fetch(step, idx_a, 0):
            copy.wait()
        for copy in fetch(step + 1, idx_b, 1):
            copy.start()

    @pl.when(jnp.logical_not(even))
    def _():
        for copy in fetch(step, idx_b, 1):
            copy.wait()

    @pl.when(jnp.logical_and(jnp.logical_not(even), step < pairs - 1))
    def _():
        for copy in fetch(step + 1, idx_a, 0):
            copy.start()

    @pl.when(step == 0)
    def _():
        gather(idx_a, buf_a)

    @pl.when(jnp.logical_and(even, jnp.logical_and(step > 0, step < pairs)))
    def _():
        gather(idx_a, buf_a)
        multiply(buf_b)

    @pl.when(jnp.logical_not(even))
    def _():
        gather(idx_b, buf_b)
        multiply(buf_a)

    @pl.when(step == pairs)
    def _():
        multiply(buf_b)
        fine_out[...] = jnp.transpose(acc[:boxes, :])
        coarse_out[...] = acc[boxes:, :]


def translate(idx, slots, poles, up_operators, far_operators, blocks):
    offsets, targets = idx.shape
    surface, boxes = blocks[0].shape
    sections = len(blocks)
    coarse = targets - boxes
    rows = sections * boxes + coarse + 8
    whole = lambda *shape: pl.BlockSpec(shape, lambda step: (0,) * len(shape))
    return pl.pallas_call(
        functools.partial(translate_kernel, sections),
        grid=(offsets // 2 + 1,),
        in_specs=[
            pl.BlockSpec(memory_space=pl.ANY),
            whole(*slots.shape),
            whole(*poles.shape),
            whole(*up_operators.shape),
            pl.BlockSpec((2, surface, surface), lambda step: (jnp.maximum(step - 1, 0), 0, 0)),
        ]
        + [whole(surface, boxes) for _ in blocks],
        out_specs=[whole(surface, boxes), whole(coarse, surface)],
        out_shape=[
            jax.ShapeDtypeStruct((surface, boxes), jnp.float32),
            jax.ShapeDtypeStruct((coarse, surface), jnp.float32),
        ],
        scratch_shapes=[
            pltpu.VMEM((2 * rows, LANES), jnp.float32),
            pltpu.VMEM((2, 2 * targets, LANES), jnp.float32),
            pltpu.VMEM((2, 2 * targets, LANES), jnp.float32),
            pltpu.VMEM((targets, surface), jnp.float32),
            pltpu.VMEM((2, poles.shape[0], LANES), jnp.float32),
            pltpu.SMEM((2, targets), jnp.int32),
            pltpu.SMEM((2, targets), jnp.int32),
            pltpu.SemaphoreType.DMA((2, 2)),
        ],
        compiler_params=pltpu.CompilerParams(vmem_limit_bytes=48 << 20),
        name="translate",
    )(idx, slots, poles, up_operators, far_operators, *blocks)


def shards(fine_mult, up_operators, far_operators, far_list, ghost_list, coarse_list):
    surface, boxes = fine_mult.shape
    bits_y = lax.axis_size("hy").bit_length() - 1
    bits_x = lax.axis_size("hx").bit_length() - 1
    blocks = [fine_mult]
    for bit_number in range(bits_y):
        blocks.append(from_partner(fine_mult, "hy", bit_number))
    for bit_number in range(bits_x):
        blocks.append(from_partner(fine_mult, "hx", bit_number))
    sections = len(blocks)
    multipoles = upward(fine_mult, up_operators)
    poles = lax.all_gather(multipoles, ("hx", "hy"), axis=0, tiled=True)
    coarse_boxes = coarse_list.shape[1]
    first_coarse = sections * boxes
    zero_row = first_coarse + coarse_boxes
    idx = jnp.concatenate(
        [
            2 * jnp.where(far_list < 0, zero_row, far_list),
            2 * jnp.where(coarse_list < 0, zero_row, coarse_list + first_coarse),
        ],
        axis=1,
    )
    slots = jnp.concatenate([jnp.arange(boxes, dtype=jnp.int32)[:, None], jnp.transpose(ghost_list[0])], axis=1)
    fine_check, coarse_check = translate(idx, slots, poles, up_operators, far_operators, blocks)
    return (fine_check, jnp.transpose(coarse_check))


def solution(mesh):
    placed = (
        P(None, ("hx", "hy")),
        P(),
        P(),
        P(None, ("hx", "hy")),
        P(("hx", "hy"), None, None),
        P(),
    )
    return jax.shard_map(
        shards, mesh=mesh, in_specs=placed, out_specs=(P(None, ("hx", "hy")), P()), check_vma=False
    )
```

```python
import functools

import jax
import jax.numpy as jnp
from jax import lax
from jax.experimental import pallas as pl
from jax.experimental.pallas import tpu as pltpu
from jax.sharding import PartitionSpec as P

LEVELS = 3
LANES = 128
NT = (((1,), (1,)), ((), ()))


def from_partner(value, axis, stride):
    mask = 2**stride
    pairs = [(source, source ^ mask) for source in range(lax.axis_size(axis))]
    return lax.ppermute(value, axis, pairs)


def lift(rows, up_ref):
    surface = up_ref.shape[1]
    count = rows.shape[1] // 8
    total = None
    for octant in range(8):
        children = jnp.concatenate([rows[half, pl.ds(octant, count, stride=8), :] for half in range(2)], axis=1)
        children = children[:, :surface].astype(jnp.bfloat16)
        term = lax.dot_general(children, up_ref[octant], NT, preferred_element_type=jnp.float32)
        total = term if total is None else total + term
    return total


def upward_kernel(place_ref, fine_ref, up_ref, out_ref, *levels):
    surface, boxes = fine_ref.shape
    spot = lax.broadcasted_iota(jnp.int32, (boxes, boxes), 0) == lax.broadcasted_iota(jnp.int32, (boxes, boxes), 1)
    rows = lax.dot_general(
        spot.astype(jnp.float32).astype(jnp.bfloat16), fine_ref[...], NT, preferred_element_type=jnp.float32
    )
    for level in levels:
        level[0] = rows[:, :LANES]
        level[1, :, : surface - LANES] = rows[:, LANES:]
        rows = lift(level, up_ref).astype(jnp.bfloat16)
        rows = rows.astype(jnp.float32)
    octant = up_ref[place_ref[1]]
    term = lax.dot_general(rows.astype(jnp.bfloat16), octant, NT, preferred_element_type=jnp.float32)
    mine = lax.broadcasted_iota(jnp.int32, out_ref.shape, 0) == place_ref[0]
    out_ref[...] = jnp.where(mine, jnp.broadcast_to(term, out_ref.shape), 0.0)


def upward(place, coarse, fine_mult, up_operators):
    surface, boxes = fine_mult.shape
    vmem = pl.BlockSpec(memory_space=pltpu.VMEM)
    return pl.pallas_call(
        upward_kernel,
        in_specs=[pl.BlockSpec(memory_space=pltpu.SMEM), vmem, vmem],
        out_specs=vmem,
        out_shape=jax.ShapeDtypeStruct((coarse, surface), jnp.float32),
        scratch_shapes=[pltpu.VMEM((2, boxes // 8**level, LANES), jnp.float32) for level in range(LEVELS)],
        name="upward",
    )(place, fine_mult, up_operators)


PAIRS = 4
CHUNKS = 2


def translate_kernel(sections, idx_hbm, slots_ref, coarse_ref, far_ref, *rest):
    blocks = rest[:sections]
    fine_out, coarse_out, table, buf_a, buf_b, acc, *rest = rest[sections:]
    idx, sem = rest[:PAIRS], rest[PAIRS]
    bufs = (buf_a, buf_b)
    step = pl.program_id(0)
    last = pl.num_programs(0) - 1
    surface = far_ref.shape[1]
    boxes = blocks[0].shape[1]
    targets = acc.shape[0]
    tail = surface - LANES
    pairs = idx_hbm.shape[0] // 2

    def fetch(pair, slot):
        pair = jnp.minimum(pair, pairs - 1)
        return [
            pltpu.make_async_copy(idx_hbm.at[2 * pair + k], idx[slot].at[k], sem.at[slot, k]) for k in range(2)
        ]

    def start(pair, slot):
        for copy in fetch(pair, slot):
            copy.start()

    def wait(slot):
        for copy in fetch(0, slot):
            copy.wait()

    def put(first, rows):
        count = rows.shape[0]
        table[pl.ds(2 * first, count, stride=2), :] = rows[:, :LANES]
        table[pl.ds(2 * first + 1, count, stride=2), :] = jnp.concatenate(
            [rows[:, LANES:], jnp.zeros((count, LANES - tail), jnp.float32)], axis=1
        )

    def gather(where, buf, part=0, parts=1):
        size = targets // parts
        for k in range(2):
            for target in range(part * size, (part + 1) * size):
                buf[k, 2 * target : 2 * target + 2, :] = table[pl.ds(where[k, target], 2), :]

    def both(where, into, buf, pair):
        weights = []
        for k in range(2):
            weights += [far_ref[2 * pair + k], jnp.zeros((surface, LANES - tail), jnp.bfloat16)]
        weights = jnp.concatenate(weights, axis=1)
        size = targets // CHUNKS
        for part in range(CHUNKS):
            rows = []
            for k in range(2):
                rows += [buf[k, pl.ds(2 * part * size + half, size, stride=2), :] for half in range(2)]
            rows = jnp.concatenate([piece.astype(jnp.bfloat16) for piece in rows], axis=1)
            span = pl.ds(part * size, size)
            acc[span, :] += lax.dot_general(rows, weights, NT, preferred_element_type=jnp.float32)
            if where is not None:
                gather(where, into, part, CHUNKS)

    @pl.when(step == 0)
    def _():
        for slot in range(PAIRS):
            start(slot, slot)
        acc[...] = jnp.zeros_like(acc)
        number = lax.broadcasted_iota(jnp.int32, (boxes, boxes), 1)
        for section in range(sections):
            spot = (slots_ref[:, section : section + 1] == number).astype(jnp.float32).astype(jnp.bfloat16)
            put(
                section * boxes,
                lax.dot_general(spot, blocks[section][...], NT, preferred_element_type=jnp.float32),
            )
        put(sections * boxes, coarse_ref[...].astype(jnp.bfloat16).astype(jnp.float32))
        put(sections * boxes + coarse_ref.shape[0], jnp.zeros((8, surface), jnp.float32))
        wait(0)
        gather(idx[0], buf_a)
        start(PAIRS, 0)

    for pair in range(PAIRS - 1):
        slot = pair + 1
        wait(slot)

        @pl.when(step <= last)
        def _():
            both(idx[slot], bufs[slot % 2], bufs[pair % 2], pair)

        start(PAIRS * (step + 1) + slot, slot)

    @pl.when(step < last)
    def _():
        wait(0)

    @pl.when(step < last)
    def _():
        both(idx[0], bufs[0], bufs[1], PAIRS - 1)

    @pl.when(step < last)
    def _():
        start(PAIRS * (step + 2), 0)

    @pl.when(step == last)
    def _():
        both(None, None, bufs[1], PAIRS - 1)
        for slot in range(PAIRS):
            wait(slot)
        fine_out[...] = jnp.transpose(acc[:boxes, :])
        coarse_out[...] = acc[boxes:, :]


def translate(idx, slots, coarse, far_operators, blocks):
    offsets, targets = idx.shape
    surface, boxes = blocks[0].shape
    sections = len(blocks)
    rows = sections * boxes + coarse.shape[0] + 8
    whole = lambda *shape: pl.BlockSpec(shape, lambda step: (0,) * len(shape))
    return pl.pallas_call(
        functools.partial(translate_kernel, sections),
        grid=(offsets // (2 * PAIRS),),
        in_specs=[
            pl.BlockSpec(memory_space=pl.ANY),
            whole(*slots.shape),
            whole(*coarse.shape),
            pl.BlockSpec((2 * PAIRS, surface, surface), lambda step: (step, 0, 0)),
        ]
        + [whole(surface, boxes) for _ in blocks],
        out_specs=[whole(surface, boxes), whole(*coarse.shape)],
        out_shape=[
            jax.ShapeDtypeStruct((surface, boxes), jnp.float32),
            jax.ShapeDtypeStruct(coarse.shape, jnp.float32),
        ],
        scratch_shapes=[
            pltpu.VMEM((2 * rows, LANES), jnp.float32),
            pltpu.VMEM((2, 2 * targets, LANES), jnp.float32),
            pltpu.VMEM((2, 2 * targets, LANES), jnp.float32),
            pltpu.VMEM((targets, surface), jnp.float32),
        ]
        + [pltpu.SMEM((2, targets), jnp.int32) for _ in range(PAIRS)]
        + [pltpu.SemaphoreType.DMA((PAIRS, 2))],
        compiler_params=pltpu.CompilerParams(vmem_limit_bytes=48 << 20),
        name="translate",
    )(idx, slots, coarse, far_operators, *blocks)


def shards(fine_mult, up_operators, far_operators, far_list, ghost_list, coarse_list):
    surface, boxes = fine_mult.shape
    bits_y = lax.axis_size("hy").bit_length() - 1
    bits_x = lax.axis_size("hx").bit_length() - 1
    coarse_boxes = coarse_list.shape[1]
    bits = [("hy", bit) for bit in range(bits_y)] + [("hx", bit) for bit in range(bits_x)]
    order = bits[bits_y : bits_y + 3][::-1] + bits[bits_y + 3 :][::-1] + bits[:bits_y][::-1]
    ghosts = {bit: from_partner(fine_mult, *bit) for bit in order}
    blocks = [fine_mult] + [ghosts[bit] for bit in bits]
    sections = len(blocks)
    place = jnp.stack([lax.axis_index("hx"), lax.axis_index("hy")]).astype(jnp.int32)
    coarse = upward(place, coarse_boxes, fine_mult, up_operators)
    for bit in bits:
        coarse = coarse + from_partner(coarse, *bit)
    first_coarse = sections * boxes
    zero_row = first_coarse + coarse_boxes
    idx = jnp.concatenate(
        [
            2 * jnp.where(far_list < 0, zero_row, far_list),
            2 * jnp.where(coarse_list < 0, zero_row, coarse_list + first_coarse),
        ],
        axis=1,
    )
    slots = jnp.concatenate([jnp.arange(boxes, dtype=jnp.int32)[:, None], jnp.transpose(ghost_list[0])], axis=1)
    fine_check, coarse_check = translate(idx, slots, coarse, far_operators, blocks)
    return (fine_check, jnp.transpose(coarse_check))


def solution(mesh):
    placed = (
        P(None, ("hx", "hy")),
        P(),
        P(),
        P(None, ("hx", "hy")),
        P(("hx", "hy"), None, None),
        P(),
    )
    return jax.shard_map(
        shards, mesh=mesh, in_specs=placed, out_specs=(P(None, ("hx", "hy")), P()), check_vma=False
    )
```

```python
import functools

import jax
import jax.numpy as jnp
from jax import lax
from jax.experimental import pallas as pl
from jax.experimental.pallas import tpu as pltpu
from jax.sharding import PartitionSpec as P

LEVELS = 3
LANES = 128
NT = (((1,), (1,)), ((), ()))


def from_partner(value, axis, stride):
    mask = 2**stride
    pairs = [(source, source ^ mask) for source in range(lax.axis_size(axis))]
    return lax.ppermute(value, axis, pairs)


def lift(rows, up_ref):
    surface = up_ref.shape[1]
    count = rows.shape[1] // 8
    total = None
    for octant in range(8):
        children = jnp.concatenate([rows[half, pl.ds(octant, count, stride=8), :] for half in range(2)], axis=1)
        children = children[:, :surface].astype(jnp.bfloat16)
        term = lax.dot_general(children, up_ref[octant], NT, preferred_element_type=jnp.float32)
        total = term if total is None else total + term
    return total


def upward_kernel(place_ref, fine_ref, up_ref, out_ref, *levels):
    surface, boxes = fine_ref.shape
    spot = lax.broadcasted_iota(jnp.int32, (boxes, boxes), 0) == lax.broadcasted_iota(jnp.int32, (boxes, boxes), 1)
    rows = lax.dot_general(
        spot.astype(jnp.float32).astype(jnp.bfloat16), fine_ref[...], NT, preferred_element_type=jnp.float32
    )
    for level in levels:
        level[0] = rows[:, :LANES]
        level[1, :, : surface - LANES] = rows[:, LANES:]
        rows = lift(level, up_ref).astype(jnp.bfloat16)
        rows = rows.astype(jnp.float32)
    octant = up_ref[place_ref[1]]
    term = lax.dot_general(rows.astype(jnp.bfloat16), octant, NT, preferred_element_type=jnp.float32)
    mine = lax.broadcasted_iota(jnp.int32, out_ref.shape, 0) == place_ref[0]
    out_ref[...] = jnp.where(mine, jnp.broadcast_to(term, out_ref.shape), 0.0)


def upward(place, coarse, fine_mult, up_operators):
    surface, boxes = fine_mult.shape
    vmem = pl.BlockSpec(memory_space=pltpu.VMEM)
    return pl.pallas_call(
        upward_kernel,
        in_specs=[pl.BlockSpec(memory_space=pltpu.SMEM), vmem, vmem],
        out_specs=vmem,
        out_shape=jax.ShapeDtypeStruct((coarse, surface), jnp.float32),
        scratch_shapes=[pltpu.VMEM((2, boxes // 8**level, LANES), jnp.float32) for level in range(LEVELS)],
        name="upward",
    )(place, fine_mult, up_operators)


STRIP = 16
PIECE = 32
GROUP = 2
PHASES = 8
CHUNKS = 2


def relayout_kernel(far_ref, out_ref, low, high):
    rows, surface, offsets = far_ref.shape
    pitch = low.shape[0] // offsets
    spot = lax.broadcasted_iota(jnp.int32, (offsets, offsets), 0) == lax.broadcasted_iota(
        jnp.int32, (offsets, offsets), 1
    )
    spot = spot.astype(jnp.float32).astype(jnp.bfloat16)
    gap = jnp.zeros((offsets, 2 * LANES - surface), jnp.float32)
    for row in range(rows):
        turned = lax.dot_general(spot, far_ref[row], NT, preferred_element_type=jnp.float32)
        low[pl.ds(row, offsets, stride=pitch), :] = turned[:, :LANES]
        high[pl.ds(row, offsets, stride=pitch), :] = jnp.concatenate([turned[:, LANES:], gap], axis=1)
    for offset in range(offsets):
        span = pl.ds(offset * pitch, rows)
        out_ref[offset, :, :LANES] = low[span, :].astype(jnp.bfloat16)
        out_ref[offset, :, LANES:] = high[span, :][:, : surface - LANES].astype(jnp.bfloat16)


def relayout(far_turned, piece):
    surface, _, offsets = far_turned.shape
    count = min(PIECE, surface - piece * PIECE)
    first = piece * PIECE // STRIP
    return pl.pallas_call(
        relayout_kernel,
        grid=(-(-count // STRIP),),
        in_specs=[pl.BlockSpec((STRIP, surface, offsets), lambda step: (first + step, 0, 0))],
        out_specs=pl.BlockSpec((offsets, STRIP, surface), lambda step: (0, step, 0)),
        out_shape=jax.ShapeDtypeStruct((offsets, count, surface), jnp.bfloat16),
        scratch_shapes=[pltpu.VMEM((offsets * (STRIP + 1), LANES), jnp.float32) for _ in range(2)],
        compiler_params=pltpu.CompilerParams(vmem_limit_bytes=16 << 20),
        cost_estimate=pl.CostEstimate(
            flops=2 * offsets * offsets * count * surface, bytes_accessed=6 * offsets * count * surface, transcendentals=0
        ),
        name="relayout",
    )(far_turned)


def add_kernel(a_ref, b_ref, *rest):
    rest[-1][...] = a_ref[...] + b_ref[...]


def add_after(a, b, others):
    vmem = pl.BlockSpec(memory_space=pltpu.VMEM)
    return pl.pallas_call(
        add_kernel,
        in_specs=[vmem, vmem] + [pl.BlockSpec(memory_space=pl.ANY) for _ in others],
        out_specs=vmem,
        out_shape=jax.ShapeDtypeStruct(a.shape, a.dtype),
        cost_estimate=pl.CostEstimate(flops=a.size, bytes_accessed=12 * a.size, transcendentals=0),
        name="add",
    )(a, b, *others)


def translate_kernel(sections, pieces, idx_hbm, slots_ref, coarse_ref, *rest):
    far_refs, rest = rest[:pieces], rest[pieces:]
    blocks = rest[:sections]
    fine_out, coarse_out, table, buf_a, buf_b, acc, *rest = rest[sections:]
    idx, sem = rest[:PHASES], rest[PHASES]
    bufs = (buf_a, buf_b)
    step = pl.program_id(0)
    last = pl.num_programs(0) - 1
    surface = far_refs[0].shape[2]
    boxes = blocks[0].shape[1]
    targets = acc.shape[0]
    tail = surface - LANES
    groups = idx_hbm.shape[0] // GROUP

    def fetch(pair, slot):
        pair = jnp.minimum(pair, groups - 1)
        return [
            pltpu.make_async_copy(idx_hbm.at[GROUP * pair + k], idx[slot].at[k], sem.at[slot, k]) for k in range(GROUP)
        ]

    def start(pair, slot):
        for copy in fetch(pair, slot):
            copy.start()

    def wait(slot):
        for copy in fetch(0, slot):
            copy.wait()

    def put(first, rows):
        count = rows.shape[0]
        table[pl.ds(2 * first, count, stride=2), :] = rows[:, :LANES]
        table[pl.ds(2 * first + 1, count, stride=2), :] = jnp.concatenate(
            [rows[:, LANES:], jnp.zeros((count, LANES - tail), jnp.float32)], axis=1
        )

    def gather(where, buf, part=0, parts=1):
        size = targets // parts
        for k in range(GROUP):
            for target in range(part * size, (part + 1) * size):
                buf[k, 2 * target : 2 * target + 2, :] = table[pl.ds(where[k, target], 2), :]

    def both(where, into, buf, pair):
        weights = []
        for k in range(GROUP):
            operator = jnp.concatenate([far_ref[GROUP * pair + k] for far_ref in far_refs], axis=0)
            weights += [operator, jnp.zeros((surface, LANES - tail), jnp.bfloat16)]
        weights = jnp.concatenate(weights, axis=1)
        size = targets // CHUNKS
        for part in range(CHUNKS):
            rows = []
            for k in range(GROUP):
                rows += [buf[k, pl.ds(2 * part * size + half, size, stride=2), :] for half in range(2)]
            rows = jnp.concatenate([piece.astype(jnp.bfloat16) for piece in rows], axis=1)
            span = pl.ds(part * size, size)
            acc[span, :] += lax.dot_general(rows, weights, NT, preferred_element_type=jnp.float32)
            if where is not None:
                gather(where, into, part, CHUNKS)

    @pl.when(step == 0)
    def _():
        for slot in range(PHASES):
            start(slot, slot)
        acc[...] = jnp.zeros_like(acc)
        number = lax.broadcasted_iota(jnp.int32, (boxes, boxes), 1)
        for section in range(sections):
            spot = (slots_ref[:, section : section + 1] == number).astype(jnp.float32).astype(jnp.bfloat16)
            put(
                section * boxes,
                lax.dot_general(spot, blocks[section][...], NT, preferred_element_type=jnp.float32),
            )
        put(sections * boxes, coarse_ref[...].astype(jnp.bfloat16).astype(jnp.float32))
        put(sections * boxes + coarse_ref.shape[0], jnp.zeros((8, surface), jnp.float32))
        wait(0)
        gather(idx[0], buf_a)
        start(PHASES, 0)

    for pair in range(PHASES - 1):
        slot = pair + 1
        wait(slot)

        @pl.when(step <= last)
        def _():
            both(idx[slot], bufs[slot % 2], bufs[pair % 2], pair)

        start(PHASES * (step + 1) + slot, slot)

    @pl.when(step < last)
    def _():
        wait(0)

    @pl.when(step < last)
    def _():
        both(idx[0], bufs[0], bufs[1], PHASES - 1)

    @pl.when(step < last)
    def _():
        start(PHASES * (step + 2), 0)

    @pl.when(step == last)
    def _():
        both(None, None, bufs[1], PHASES - 1)
        for slot in range(PHASES):
            wait(slot)
        fine_out[...] = jnp.transpose(acc[:boxes, :])
        coarse_out[...] = acc[boxes:, :]


def translate(idx, slots, coarse, far_pieces, blocks):
    offsets, targets = idx.shape
    surface, boxes = blocks[0].shape
    sections = len(blocks)
    rows = sections * boxes + coarse.shape[0] + 8
    whole = lambda *shape: pl.BlockSpec(shape, lambda step: (0,) * len(shape))
    return pl.pallas_call(
        functools.partial(translate_kernel, sections, len(far_pieces)),
        grid=(offsets // (GROUP * PHASES),),
        in_specs=[
            pl.BlockSpec(memory_space=pl.ANY),
            whole(*slots.shape),
            whole(*coarse.shape),
        ]
        + [pl.BlockSpec((GROUP * PHASES, *piece.shape[1:]), lambda step: (step, 0, 0)) for piece in far_pieces]
        + [whole(surface, boxes) for _ in blocks],
        out_specs=[whole(surface, boxes), whole(*coarse.shape)],
        out_shape=[
            jax.ShapeDtypeStruct((surface, boxes), jnp.float32),
            jax.ShapeDtypeStruct(coarse.shape, jnp.float32),
        ],
        scratch_shapes=[
            pltpu.VMEM((2 * rows, LANES), jnp.float32),
            pltpu.VMEM((GROUP, 2 * targets, LANES), jnp.float32),
            pltpu.VMEM((GROUP, 2 * targets, LANES), jnp.float32),
            pltpu.VMEM((targets, surface), jnp.float32),
        ]
        + [pltpu.SMEM((GROUP, targets), jnp.int32) for _ in range(PHASES)]
        + [pltpu.SemaphoreType.DMA((PHASES, GROUP))],
        compiler_params=pltpu.CompilerParams(vmem_limit_bytes=48 << 20),
        name="translate",
    )(idx, slots, coarse, *far_pieces, *blocks)


def shards(fine_mult, up_operators, far_operators, far_list, ghost_list, coarse_list):
    surface, boxes = fine_mult.shape
    bits_y = lax.axis_size("hy").bit_length() - 1
    bits_x = lax.axis_size("hx").bit_length() - 1
    coarse_boxes = coarse_list.shape[1]
    bits = [("hy", bit) for bit in range(bits_y)] + [("hx", bit) for bit in range(bits_x)]
    order = bits[bits_y : bits_y + 3][::-1] + bits[bits_y + 3 :][::-1] + bits[:bits_y][::-1]
    ghosts = {bit: from_partner(fine_mult, *bit) for bit in order}
    blocks = [fine_mult] + [ghosts[bit] for bit in bits]
    sections = len(blocks)
    place = jnp.stack([lax.axis_index("hx"), lax.axis_index("hy")]).astype(jnp.int32)
    coarse = upward(place, coarse_boxes, fine_mult, up_operators)
    far_turned = jnp.transpose(far_operators, (1, 2, 0))
    pieces = [relayout(far_turned, piece) for piece in range(-(-surface // PIECE))]
    due = [[piece] for piece in pieces] + [[] for _ in range(len(bits) - len(pieces))]
    for number, bit in enumerate(order):
        due[min(4 + number // 2, len(bits) - 1)].append(ghosts[bit])
    for bit, others in zip(bits, due):
        coarse = add_after(coarse, from_partner(coarse, *bit), others)
    first_coarse = sections * boxes
    zero_row = first_coarse + coarse_boxes
    idx = jnp.concatenate(
        [
            2 * jnp.where(far_list < 0, zero_row, far_list),
            2 * jnp.where(coarse_list < 0, zero_row, coarse_list + first_coarse),
        ],
        axis=1,
    )
    slots = jnp.concatenate([jnp.arange(boxes, dtype=jnp.int32)[:, None], jnp.transpose(ghost_list[0])], axis=1)
    fine_check, coarse_check = translate(idx, slots, coarse, pieces, blocks)
    return (fine_check, jnp.transpose(coarse_check))


def solution(mesh):
    placed = (
        P(None, ("hx", "hy")),
        P(),
        P(),
        P(None, ("hx", "hy")),
        P(("hx", "hy"), None, None),
        P(),
    )
    return jax.shard_map(
        shards, mesh=mesh, in_specs=placed, out_specs=(P(None, ("hx", "hy")), P()), check_vma=False
    )
```

```python
import functools

import jax
import jax.numpy as jnp
from jax import lax
from jax.experimental import pallas as pl
from jax.experimental.pallas import tpu as pltpu
from jax.sharding import PartitionSpec as P

LEVELS = 3
LANES = 128
NT = (((1,), (1,)), ((), ()))


def from_partner(value, axis, stride):
    mask = 2**stride
    pairs = [(source, source ^ mask) for source in range(lax.axis_size(axis))]
    return lax.ppermute(value, axis, pairs)


def lift(rows, up_ref):
    surface = up_ref.shape[1]
    count = rows.shape[1] // 8
    total = None
    for octant in range(8):
        children = jnp.concatenate([rows[half, pl.ds(octant, count, stride=8), :] for half in range(2)], axis=1)
        children = children[:, :surface].astype(jnp.bfloat16)
        term = lax.dot_general(children, up_ref[octant], NT, preferred_element_type=jnp.float32)
        total = term if total is None else total + term
    return total


def upward_kernel(place_ref, fine_ref, up_ref, out_ref, *levels):
    surface, boxes = fine_ref.shape
    spot = lax.broadcasted_iota(jnp.int32, (boxes, boxes), 0) == lax.broadcasted_iota(jnp.int32, (boxes, boxes), 1)
    rows = lax.dot_general(
        spot.astype(jnp.float32).astype(jnp.bfloat16), fine_ref[...], NT, preferred_element_type=jnp.float32
    )
    for level in levels:
        level[0] = rows[:, :LANES]
        level[1, :, : surface - LANES] = rows[:, LANES:]
        rows = lift(level, up_ref).astype(jnp.bfloat16)
        rows = rows.astype(jnp.float32)
    octant = up_ref[place_ref[1]]
    term = lax.dot_general(rows.astype(jnp.bfloat16), octant, NT, preferred_element_type=jnp.float32)
    mine = lax.broadcasted_iota(jnp.int32, out_ref.shape, 0) == place_ref[0]
    out_ref[...] = jnp.where(mine, jnp.broadcast_to(term, out_ref.shape), 0.0)


def upward(place, coarse, fine_mult, up_operators):
    surface, boxes = fine_mult.shape
    vmem = pl.BlockSpec(memory_space=pltpu.VMEM)
    return pl.pallas_call(
        upward_kernel,
        in_specs=[pl.BlockSpec(memory_space=pltpu.SMEM), vmem, vmem],
        out_specs=vmem,
        out_shape=jax.ShapeDtypeStruct((coarse, surface), jnp.float32),
        scratch_shapes=[pltpu.VMEM((2, boxes // 8**level, LANES), jnp.float32) for level in range(LEVELS)],
        name="upward",
    )(place, fine_mult, up_operators)


SETTLED = 4
STRIP = 16
PIECE = 32
GROUP = 2
PHASES = 8
CHUNKS = 2


def relayout_kernel(far_ref, out_ref, low, high):
    rows, surface, offsets = far_ref.shape
    pitch = low.shape[0] // offsets
    spot = lax.broadcasted_iota(jnp.int32, (offsets, offsets), 0) == lax.broadcasted_iota(
        jnp.int32, (offsets, offsets), 1
    )
    spot = spot.astype(jnp.float32).astype(jnp.bfloat16)
    gap = jnp.zeros((offsets, 2 * LANES - surface), jnp.float32)
    for row in range(rows):
        turned = lax.dot_general(spot, far_ref[row], NT, preferred_element_type=jnp.float32)
        low[pl.ds(row, offsets, stride=pitch), :] = turned[:, :LANES]
        high[pl.ds(row, offsets, stride=pitch), :] = jnp.concatenate([turned[:, LANES:], gap], axis=1)
    for offset in range(offsets):
        span = pl.ds(offset * pitch, rows)
        out_ref[offset, :, :LANES] = low[span, :].astype(jnp.bfloat16)
        out_ref[offset, :, LANES:] = high[span, :][:, : surface - LANES].astype(jnp.bfloat16)


def relayout(far_turned, piece):
    surface, _, offsets = far_turned.shape
    count = min(PIECE, surface - piece * PIECE)
    first = piece * PIECE // STRIP
    return pl.pallas_call(
        relayout_kernel,
        grid=(-(-count // STRIP),),
        in_specs=[pl.BlockSpec((STRIP, surface, offsets), lambda step: (first + step, 0, 0))],
        out_specs=pl.BlockSpec((offsets, STRIP, surface), lambda step: (0, step, 0)),
        out_shape=jax.ShapeDtypeStruct((offsets, count, surface), jnp.bfloat16),
        scratch_shapes=[pltpu.VMEM((offsets * (STRIP + 1), LANES), jnp.float32) for _ in range(2)],
        compiler_params=pltpu.CompilerParams(vmem_limit_bytes=60 << 20),
        cost_estimate=pl.CostEstimate(
            flops=2 * offsets * offsets * count * surface, bytes_accessed=6 * offsets * count * surface, transcendentals=0
        ),
        name="relayout",
    )(far_turned)


def translate_kernel(sections, pieces, idx_hbm, slots_ref, coarse_ref, *rest):
    far_refs, rest = rest[:pieces], rest[pieces:]
    blocks = rest[:sections]
    fine_out, coarse_out, table, buf_a, buf_b, acc, *rest = rest[sections:]
    idx, sem = rest[:PHASES], rest[PHASES]
    bufs = (buf_a, buf_b)
    step = pl.program_id(0)
    last = pl.num_programs(0) - 1
    surface = far_refs[0].shape[2]
    boxes = blocks[0].shape[1]
    targets = acc.shape[0]
    tail = surface - LANES
    groups = idx_hbm.shape[0] // GROUP

    def fetch(pair, slot):
        pair = jnp.minimum(pair, groups - 1)
        return [
            pltpu.make_async_copy(idx_hbm.at[GROUP * pair + k], idx[slot].at[k], sem.at[slot, k]) for k in range(GROUP)
        ]

    def start(pair, slot):
        for copy in fetch(pair, slot):
            copy.start()

    def wait(slot):
        for copy in fetch(0, slot):
            copy.wait()

    def put(first, rows):
        count = rows.shape[0]
        table[pl.ds(2 * first, count, stride=2), :] = rows[:, :LANES]
        table[pl.ds(2 * first + 1, count, stride=2), :] = jnp.concatenate(
            [rows[:, LANES:], jnp.zeros((count, LANES - tail), jnp.float32)], axis=1
        )

    def gather(where, buf, part=0, parts=1):
        size = targets // parts
        for k in range(GROUP):
            for target in range(part * size, (part + 1) * size):
                buf[k, 2 * target : 2 * target + 2, :] = table[pl.ds(where[k, target], 2), :]

    def both(where, into, buf, pair):
        weights = []
        for k in range(GROUP):
            operator = jnp.concatenate([far_ref[GROUP * pair + k] for far_ref in far_refs], axis=0)
            weights += [operator, jnp.zeros((surface, LANES - tail), jnp.bfloat16)]
        weights = jnp.concatenate(weights, axis=1)
        size = targets // CHUNKS
        for part in range(CHUNKS):
            rows = []
            for k in range(GROUP):
                rows += [buf[k, pl.ds(2 * part * size + half, size, stride=2), :] for half in range(2)]
            rows = jnp.concatenate([piece.astype(jnp.bfloat16) for piece in rows], axis=1)
            span = pl.ds(part * size, size)
            acc[span, :] += lax.dot_general(rows, weights, NT, preferred_element_type=jnp.float32)
            if where is not None:
                gather(where, into, part, CHUNKS)

    @pl.when(step == 0)
    def _():
        for slot in range(PHASES):
            start(slot, slot)
        acc[...] = jnp.zeros_like(acc)
        number = lax.broadcasted_iota(jnp.int32, (boxes, boxes), 1)
        for section in range(sections):
            spot = (slots_ref[:, section : section + 1] == number).astype(jnp.float32).astype(jnp.bfloat16)
            put(
                section * boxes,
                lax.dot_general(spot, blocks[section][...], NT, preferred_element_type=jnp.float32),
            )
        put(sections * boxes, coarse_ref[...].astype(jnp.bfloat16).astype(jnp.float32))
        put(sections * boxes + coarse_ref.shape[0], jnp.zeros((8, surface), jnp.float32))
        wait(0)
        gather(idx[0], buf_a)
        start(PHASES, 0)

    for pair in range(PHASES - 1):
        slot = pair + 1
        wait(slot)

        @pl.when(step <= last)
        def _():
            both(idx[slot], bufs[slot % 2], bufs[pair % 2], pair)

        start(PHASES * (step + 1) + slot, slot)

    @pl.when(step < last)
    def _():
        wait(0)

    @pl.when(step < last)
    def _():
        both(idx[0], bufs[0], bufs[1], PHASES - 1)

    @pl.when(step < last)
    def _():
        start(PHASES * (step + 2), 0)

    @pl.when(step == last)
    def _():
        both(None, None, bufs[1], PHASES - 1)
        for slot in range(PHASES):
            wait(slot)
        fine_out[...] = jnp.transpose(acc[:boxes, :])
        coarse_out[...] = acc[boxes:, :]


def translate(idx, slots, coarse, far_pieces, blocks):
    offsets, targets = idx.shape
    surface, boxes = blocks[0].shape
    sections = len(blocks)
    rows = sections * boxes + coarse.shape[0] + 8
    whole = lambda *shape: pl.BlockSpec(shape, lambda step: (0,) * len(shape))
    return pl.pallas_call(
        functools.partial(translate_kernel, sections, len(far_pieces)),
        grid=(offsets // (GROUP * PHASES),),
        in_specs=[
            pl.BlockSpec(memory_space=pl.ANY),
            whole(*slots.shape),
            whole(*coarse.shape),
        ]
        + [pl.BlockSpec((GROUP * PHASES, *piece.shape[1:]), lambda step: (step, 0, 0)) for piece in far_pieces]
        + [whole(surface, boxes) for _ in blocks],
        out_specs=[whole(surface, boxes), whole(*coarse.shape)],
        out_shape=[
            jax.ShapeDtypeStruct((surface, boxes), jnp.float32),
            jax.ShapeDtypeStruct(coarse.shape, jnp.float32),
        ],
        scratch_shapes=[
            pltpu.VMEM((2 * rows, LANES), jnp.float32),
            pltpu.VMEM((GROUP, 2 * targets, LANES), jnp.float32),
            pltpu.VMEM((GROUP, 2 * targets, LANES), jnp.float32),
            pltpu.VMEM((targets, surface), jnp.float32),
        ]
        + [pltpu.SMEM((GROUP, targets), jnp.int32) for _ in range(PHASES)]
        + [pltpu.SemaphoreType.DMA((PHASES, GROUP))],
        compiler_params=pltpu.CompilerParams(vmem_limit_bytes=51 << 20),
        name="translate",
    )(idx, slots, coarse, *far_pieces, *blocks)


def shards(fine_mult, up_operators, far_operators, far_list, ghost_list, coarse_list):
    surface, boxes = fine_mult.shape
    bits_y = lax.axis_size("hy").bit_length() - 1
    bits_x = lax.axis_size("hx").bit_length() - 1
    coarse_boxes = coarse_list.shape[1]
    bits = [("hy", bit) for bit in range(bits_y)] + [("hx", bit) for bit in range(bits_x)]
    order = bits[bits_y : bits_y + 3][::-1] + bits[bits_y + 3 :][::-1] + bits[:bits_y][::-1]
    ghosts = {bit: from_partner(fine_mult, *bit) for bit in order}
    sections = len(bits) + 1
    place = jnp.stack([lax.axis_index("hx"), lax.axis_index("hy")]).astype(jnp.int32)
    coarse = upward(place, coarse_boxes, fine_mult, up_operators)
    far_turned = jnp.transpose(far_operators, (1, 2, 0))
    pieces = [relayout(far_turned, piece) for piece in range(-(-surface // PIECE))]
    for number, bit in enumerate(bits):
        coarse = coarse + from_partner(coarse, *bit)
        if number < len(pieces):
            coarse, pieces[number] = lax.optimization_barrier((coarse, pieces[number]))
        if SETTLED <= number < len(bits) - 1:
            for other in order[2 * (number - SETTLED) : 2 * (number - SETTLED) + 2]:
                coarse, ghosts[other] = lax.optimization_barrier((coarse, ghosts[other]))
    blocks = [fine_mult] + [ghosts[bit] for bit in bits]
    first_coarse = sections * boxes
    zero_row = first_coarse + coarse_boxes
    idx = jnp.concatenate(
        [
            2 * jnp.where(far_list < 0, zero_row, far_list),
            2 * jnp.where(coarse_list < 0, zero_row, coarse_list + first_coarse),
        ],
        axis=1,
    )
    slots = jnp.concatenate([jnp.arange(boxes, dtype=jnp.int32)[:, None], jnp.transpose(ghost_list[0])], axis=1)
    fine_check, coarse_check = translate(idx, slots, coarse, pieces, blocks)
    return (fine_check, jnp.transpose(coarse_check))


def solution(mesh):
    placed = (
        P(None, ("hx", "hy")),
        P(),
        P(),
        P(None, ("hx", "hy")),
        P(("hx", "hy"), None, None),
        P(),
    )
    return jax.shard_map(
        shards, mesh=mesh, in_specs=placed, out_specs=(P(None, ("hx", "hy")), P()), check_vma=False
    )
```

```python
import functools

import jax
import jax.numpy as jnp
from jax import lax
from jax.experimental import pallas as pl
from jax.experimental.pallas import tpu as pltpu
from jax.sharding import PartitionSpec as P

LEVELS = 3
LANES = 128
NT = (((1,), (1,)), ((), ()))


def from_partner(value, axis, stride):
    mask = 2**stride
    pairs = [(source, source ^ mask) for source in range(lax.axis_size(axis))]
    return lax.ppermute(value, axis, pairs)


def lift(rows, up_ref):
    surface = up_ref.shape[1]
    count = rows.shape[1] // 8
    total = None
    for octant in range(8):
        children = jnp.concatenate([rows[half, pl.ds(octant, count, stride=8), :] for half in range(2)], axis=1)
        children = children[:, :surface].astype(jnp.bfloat16)
        term = lax.dot_general(children, up_ref[octant], NT, preferred_element_type=jnp.float32)
        total = term if total is None else total + term
    return total


def upward_kernel(place_ref, fine_ref, up_ref, out_ref, *levels):
    surface, boxes = fine_ref.shape
    spot = lax.broadcasted_iota(jnp.int32, (boxes, boxes), 0) == lax.broadcasted_iota(jnp.int32, (boxes, boxes), 1)
    rows = lax.dot_general(
        spot.astype(jnp.float32).astype(jnp.bfloat16), fine_ref[...], NT, preferred_element_type=jnp.float32
    )
    for level in levels:
        level[0] = rows[:, :LANES]
        level[1, :, : surface - LANES] = rows[:, LANES:]
        rows = lift(level, up_ref).astype(jnp.bfloat16)
        rows = rows.astype(jnp.float32)
    octant = up_ref[place_ref[1]]
    term = lax.dot_general(rows.astype(jnp.bfloat16), octant, NT, preferred_element_type=jnp.float32)
    mine = lax.broadcasted_iota(jnp.int32, out_ref.shape, 0) == place_ref[0]
    out_ref[...] = jnp.where(mine, jnp.broadcast_to(term, out_ref.shape), 0.0)


def upward(place, coarse, fine_mult, up_operators):
    surface, boxes = fine_mult.shape
    vmem = pl.BlockSpec(memory_space=pltpu.VMEM)
    return pl.pallas_call(
        upward_kernel,
        in_specs=[pl.BlockSpec(memory_space=pltpu.SMEM), vmem, vmem],
        out_specs=vmem,
        out_shape=jax.ShapeDtypeStruct((coarse, surface), jnp.float32),
        scratch_shapes=[pltpu.VMEM((2, boxes // 8**level, LANES), jnp.float32) for level in range(LEVELS)],
        name="upward",
    )(place, fine_mult, up_operators)


SETTLED = 3
STRIP = 16
GROUP = 2
PHASES = 8
CHUNKS = 2


def relayout_kernel(far_ref, out_ref, low, high):
    rows, surface, offsets = far_ref.shape
    pitch = low.shape[0] // offsets
    spot = lax.broadcasted_iota(jnp.int32, (offsets, offsets), 0) == lax.broadcasted_iota(
        jnp.int32, (offsets, offsets), 1
    )
    spot = spot.astype(jnp.float32).astype(jnp.bfloat16)
    gap = jnp.zeros((offsets, 2 * LANES - surface), jnp.float32)
    for row in range(rows):
        turned = lax.dot_general(spot, far_ref[row], NT, preferred_element_type=jnp.float32)
        low[pl.ds(row, offsets, stride=pitch), :] = turned[:, :LANES]
        high[pl.ds(row, offsets, stride=pitch), :] = jnp.concatenate([turned[:, LANES:], gap], axis=1)
    for offset in range(offsets):
        span = pl.ds(offset * pitch, rows)
        out_ref[offset, :, :LANES] = low[span, :].astype(jnp.bfloat16)
        out_ref[offset, :, LANES:] = high[span, :][:, : surface - LANES].astype(jnp.bfloat16)


def relayout(far_turned, first, strips):
    surface, _, offsets = far_turned.shape
    count = min(strips * STRIP, surface - first * STRIP)
    return pl.pallas_call(
        relayout_kernel,
        grid=(strips,),
        in_specs=[pl.BlockSpec((STRIP, surface, offsets), lambda step: (first + step, 0, 0))],
        out_specs=pl.BlockSpec((offsets, STRIP, surface), lambda step: (0, step, 0)),
        out_shape=jax.ShapeDtypeStruct((offsets, count, surface), jnp.bfloat16),
        scratch_shapes=[pltpu.VMEM((offsets * (STRIP + 1), LANES), jnp.float32) for _ in range(2)],
        compiler_params=pltpu.CompilerParams(vmem_limit_bytes=60 << 20),
        cost_estimate=pl.CostEstimate(
            flops=2 * offsets * offsets * count * surface, bytes_accessed=6 * offsets * count * surface, transcendentals=0
        ),
        name="relayout",
    )(far_turned)


def translate_kernel(sections, pieces, idx_hbm, slots_ref, coarse_ref, *rest):
    far_refs, rest = rest[:pieces], rest[pieces:]
    blocks = rest[:sections]
    fine_out, coarse_out, table, buf_a, buf_b, acc, *rest = rest[sections:]
    idx, sem = rest[:PHASES], rest[PHASES]
    bufs = (buf_a, buf_b)
    step = pl.program_id(0)
    last = pl.num_programs(0) - 1
    surface = far_refs[0].shape[2]
    boxes = blocks[0].shape[1]
    targets = acc.shape[0]
    tail = surface - LANES
    groups = idx_hbm.shape[0] // GROUP

    def fetch(pair, slot):
        pair = jnp.minimum(pair, groups - 1)
        return [
            pltpu.make_async_copy(idx_hbm.at[GROUP * pair + k], idx[slot].at[k], sem.at[slot, k]) for k in range(GROUP)
        ]

    def start(pair, slot):
        for copy in fetch(pair, slot):
            copy.start()

    def wait(slot):
        for copy in fetch(0, slot):
            copy.wait()

    def put(first, rows):
        count = rows.shape[0]
        table[pl.ds(2 * first, count, stride=2), :] = rows[:, :LANES]
        table[pl.ds(2 * first + 1, count, stride=2), :] = jnp.concatenate(
            [rows[:, LANES:], jnp.zeros((count, LANES - tail), jnp.float32)], axis=1
        )

    def gather(where, buf, part=0, parts=1):
        size = targets // parts
        for k in range(GROUP):
            for target in range(part * size, (part + 1) * size):
                buf[k, 2 * target : 2 * target + 2, :] = table[pl.ds(where[k, target], 2), :]

    def both(where, into, buf, pair):
        weights = []
        for k in range(GROUP):
            operator = jnp.concatenate([far_ref[GROUP * pair + k] for far_ref in far_refs], axis=0)
            weights += [operator, jnp.zeros((surface, LANES - tail), jnp.bfloat16)]
        weights = jnp.concatenate(weights, axis=1)
        size = targets // CHUNKS
        for part in range(CHUNKS):
            rows = []
            for k in range(GROUP):
                rows += [buf[k, pl.ds(2 * part * size + half, size, stride=2), :] for half in range(2)]
            rows = jnp.concatenate([piece.astype(jnp.bfloat16) for piece in rows], axis=1)
            span = pl.ds(part * size, size)
            acc[span, :] += lax.dot_general(rows, weights, NT, preferred_element_type=jnp.float32)
            if where is not None:
                gather(where, into, part, CHUNKS)

    @pl.when(step == 0)
    def _():
        for slot in range(PHASES):
            start(slot, slot)
        acc[...] = jnp.zeros_like(acc)
        number = lax.broadcasted_iota(jnp.int32, (boxes, boxes), 1)
        for section in range(sections):
            spot = (slots_ref[:, section : section + 1] == number).astype(jnp.float32).astype(jnp.bfloat16)
            put(
                section * boxes,
                lax.dot_general(spot, blocks[section][...], NT, preferred_element_type=jnp.float32),
            )
        put(sections * boxes, coarse_ref[...].astype(jnp.bfloat16).astype(jnp.float32))
        put(sections * boxes + coarse_ref.shape[0], jnp.zeros((8, surface), jnp.float32))
        wait(0)
        gather(idx[0], buf_a)
        start(PHASES, 0)

    for pair in range(PHASES - 1):
        slot = pair + 1
        wait(slot)

        @pl.when(step <= last)
        def _():
            both(idx[slot], bufs[slot % 2], bufs[pair % 2], pair)

        start(PHASES * (step + 1) + slot, slot)

    @pl.when(step < last)
    def _():
        wait(0)

    @pl.when(step < last)
    def _():
        both(idx[0], bufs[0], bufs[1], PHASES - 1)

    @pl.when(step < last)
    def _():
        start(PHASES * (step + 2), 0)

    @pl.when(step == last)
    def _():
        both(None, None, bufs[1], PHASES - 1)
        for slot in range(PHASES):
            wait(slot)
        fine_out[...] = jnp.transpose(acc[:boxes, :])
        coarse_out[...] = acc[boxes:, :]


def translate(idx, slots, coarse, far_pieces, blocks):
    offsets, targets = idx.shape
    surface, boxes = blocks[0].shape
    sections = len(blocks)
    rows = sections * boxes + coarse.shape[0] + 8
    whole = lambda *shape: pl.BlockSpec(shape, lambda step: (0,) * len(shape))
    return pl.pallas_call(
        functools.partial(translate_kernel, sections, len(far_pieces)),
        grid=(offsets // (GROUP * PHASES),),
        in_specs=[
            pl.BlockSpec(memory_space=pl.ANY),
            whole(*slots.shape),
            whole(*coarse.shape),
        ]
        + [pl.BlockSpec((GROUP * PHASES, *piece.shape[1:]), lambda step: (step, 0, 0)) for piece in far_pieces]
        + [whole(surface, boxes) for _ in blocks],
        out_specs=[whole(surface, boxes), whole(*coarse.shape)],
        out_shape=[
            jax.ShapeDtypeStruct((surface, boxes), jnp.float32),
            jax.ShapeDtypeStruct(coarse.shape, jnp.float32),
        ],
        scratch_shapes=[
            pltpu.VMEM((2 * rows, LANES), jnp.float32),
            pltpu.VMEM((GROUP, 2 * targets, LANES), jnp.float32),
            pltpu.VMEM((GROUP, 2 * targets, LANES), jnp.float32),
            pltpu.VMEM((targets, surface), jnp.float32),
        ]
        + [pltpu.SMEM((GROUP, targets), jnp.int32) for _ in range(PHASES)]
        + [pltpu.SemaphoreType.DMA((PHASES, GROUP))],
        compiler_params=pltpu.CompilerParams(vmem_limit_bytes=51 << 20),
        name="translate",
    )(idx, slots, coarse, *far_pieces, *blocks)


def shards(fine_mult, up_operators, far_operators, far_list, ghost_list, coarse_list):
    surface, boxes = fine_mult.shape
    bits_y = lax.axis_size("hy").bit_length() - 1
    bits_x = lax.axis_size("hx").bit_length() - 1
    coarse_boxes = coarse_list.shape[1]
    bits = [("hy", bit) for bit in range(bits_y)] + [("hx", bit) for bit in range(bits_x)]
    order = bits[bits_y : bits_y + 3][::-1] + bits[bits_y + 3 :][::-1] + bits[:bits_y][::-1]
    ghosts = {bit: from_partner(fine_mult, *bit) for bit in order}
    sections = len(bits) + 1
    place = jnp.stack([lax.axis_index("hx"), lax.axis_index("hy")]).astype(jnp.int32)
    coarse = upward(place, coarse_boxes, fine_mult, up_operators)
    far_turned = jnp.transpose(far_operators, (1, 2, 0))
    strips = -(-surface // STRIP)
    cuts = [stage * strips // len(bits) for stage in range(len(bits) + 1)]
    pieces = [relayout(far_turned, low, high - low) for low, high in zip(cuts, cuts[1:])]
    stages = [bit for bit in bits if bit != order[0]] + [order[0]]
    for number, bit in enumerate(stages):
        coarse = coarse + from_partner(coarse, *bit)
        coarse, pieces[number] = lax.optimization_barrier((coarse, pieces[number]))
        if SETTLED <= number < len(stages) - 1:
            for other in order[2 * (number - SETTLED) : 2 * (number - SETTLED) + 2]:
                coarse, ghosts[other] = lax.optimization_barrier((coarse, ghosts[other]))
    blocks = [fine_mult] + [ghosts[bit] for bit in bits]
    first_coarse = sections * boxes
    zero_row = first_coarse + coarse_boxes
    idx = jnp.concatenate(
        [
            2 * jnp.where(far_list < 0, zero_row, far_list),
            2 * jnp.where(coarse_list < 0, zero_row, coarse_list + first_coarse),
        ],
        axis=1,
    )
    slots = jnp.concatenate([jnp.arange(boxes, dtype=jnp.int32)[:, None], jnp.transpose(ghost_list[0])], axis=1)
    fine_check, coarse_check = translate(idx, slots, coarse, pieces, blocks)
    return (fine_check, jnp.transpose(coarse_check))


def solution(mesh):
    placed = (
        P(None, ("hx", "hy")),
        P(),
        P(),
        P(None, ("hx", "hy")),
        P(("hx", "hy"), None, None),
        P(),
    )
    return jax.shard_map(
        shards, mesh=mesh, in_specs=placed, out_specs=(P(None, ("hx", "hy")), P()), check_vma=False
    )
```

```python
import functools

import jax
import jax.numpy as jnp
from jax import lax
from jax.experimental import pallas as pl
from jax.experimental.pallas import tpu as pltpu
from jax.sharding import PartitionSpec as P

LEVELS = 3
LANES = 128
NT = (((1,), (1,)), ((), ()))


def from_partner(value, axis, stride):
    mask = 2**stride
    pairs = [(source, source ^ mask) for source in range(lax.axis_size(axis))]
    return lax.ppermute(value, axis, pairs)


def lift(rows, up_ref):
    surface = up_ref.shape[1]
    count = rows.shape[1] // 8
    total = None
    for octant in range(8):
        children = jnp.concatenate([rows[half, pl.ds(octant, count, stride=8), :] for half in range(2)], axis=1)
        children = children[:, :surface].astype(jnp.bfloat16)
        term = lax.dot_general(children, up_ref[octant], NT, preferred_element_type=jnp.float32)
        total = term if total is None else total + term
    return total


def upward_kernel(place_ref, fine_ref, up_ref, out_ref, *levels):
    surface, boxes = fine_ref.shape
    spot = lax.broadcasted_iota(jnp.int32, (boxes, boxes), 0) == lax.broadcasted_iota(jnp.int32, (boxes, boxes), 1)
    rows = lax.dot_general(
        spot.astype(jnp.float32).astype(jnp.bfloat16), fine_ref[...], NT, preferred_element_type=jnp.float32
    )
    for level in levels:
        level[0] = rows[:, :LANES]
        level[1, :, : surface - LANES] = rows[:, LANES:]
        rows = lift(level, up_ref).astype(jnp.bfloat16)
        rows = rows.astype(jnp.float32)
    octant = up_ref[place_ref[1]]
    term = lax.dot_general(rows.astype(jnp.bfloat16), octant, NT, preferred_element_type=jnp.float32)
    mine = lax.broadcasted_iota(jnp.int32, out_ref.shape, 0) == place_ref[0]
    out_ref[...] = jnp.where(mine, jnp.broadcast_to(term, out_ref.shape), 0.0)


def upward(place, coarse, fine_mult, up_operators):
    surface, boxes = fine_mult.shape
    vmem = pl.BlockSpec(memory_space=pltpu.VMEM)
    return pl.pallas_call(
        upward_kernel,
        in_specs=[pl.BlockSpec(memory_space=pltpu.SMEM), vmem, vmem],
        out_specs=vmem,
        out_shape=jax.ShapeDtypeStruct((coarse, surface), jnp.float32),
        scratch_shapes=[pltpu.VMEM((2, boxes // 8**level, LANES), jnp.float32) for level in range(LEVELS)],
        name="upward",
    )(place, fine_mult, up_operators)


SETTLED = 3
STRIP = 16
GROUP = 2
PHASES = 16
CHUNKS = 2


def relayout_kernel(far_ref, out_ref, low, high):
    rows, surface, offsets = far_ref.shape
    pitch = low.shape[0] // offsets
    spot = lax.broadcasted_iota(jnp.int32, (offsets, offsets), 0) == lax.broadcasted_iota(
        jnp.int32, (offsets, offsets), 1
    )
    spot = spot.astype(jnp.float32).astype(jnp.bfloat16)
    gap = jnp.zeros((offsets, 2 * LANES - surface), jnp.float32)
    for row in range(rows):
        turned = lax.dot_general(spot, far_ref[row], NT, preferred_element_type=jnp.float32)
        low[pl.ds(row, offsets, stride=pitch), :] = turned[:, :LANES]
        high[pl.ds(row, offsets, stride=pitch), :] = jnp.concatenate([turned[:, LANES:], gap], axis=1)
    for offset in range(offsets):
        span = pl.ds(offset * pitch, rows)
        out_ref[offset, :, :LANES] = low[span, :].astype(jnp.bfloat16)
        out_ref[offset, :, LANES:] = high[span, :][:, : surface - LANES].astype(jnp.bfloat16)


def relayout(far_turned, first, strips):
    surface, _, offsets = far_turned.shape
    count = min(strips * STRIP, surface - first * STRIP)
    return pl.pallas_call(
        relayout_kernel,
        grid=(strips,),
        in_specs=[pl.BlockSpec((STRIP, surface, offsets), lambda step: (first + step, 0, 0))],
        out_specs=pl.BlockSpec((offsets, STRIP, surface), lambda step: (0, step, 0)),
        out_shape=jax.ShapeDtypeStruct((offsets, count, surface), jnp.bfloat16),
        scratch_shapes=[pltpu.VMEM((offsets * (STRIP + 1), LANES), jnp.float32) for _ in range(2)],
        compiler_params=pltpu.CompilerParams(vmem_limit_bytes=60 << 20),
        cost_estimate=pl.CostEstimate(
            flops=2 * offsets * offsets * count * surface, bytes_accessed=6 * offsets * count * surface, transcendentals=0
        ),
        name="relayout",
    )(far_turned)


def translate_kernel(sections, pieces, idx_hbm, slots_ref, coarse_ref, *rest):
    far_refs, rest = rest[:pieces], rest[pieces:]
    blocks = rest[:sections]
    fine_out, coarse_out, table, buf_a, buf_b, acc, *rest = rest[sections:]
    idx, sem = rest[:PHASES], rest[PHASES]
    bufs = (buf_a, buf_b)
    step = pl.program_id(0)
    last = pl.num_programs(0) - 1
    surface = far_refs[0].shape[2]
    boxes = blocks[0].shape[1]
    targets = acc.shape[0]
    tail = surface - LANES
    groups = idx_hbm.shape[0] // GROUP

    def fetch(pair, slot):
        pair = jnp.minimum(pair, groups - 1)
        return [
            pltpu.make_async_copy(idx_hbm.at[GROUP * pair + k], idx[slot].at[k], sem.at[slot, k]) for k in range(GROUP)
        ]

    def start(pair, slot):
        for copy in fetch(pair, slot):
            copy.start()

    def wait(slot):
        for copy in fetch(0, slot):
            copy.wait()

    def put(first, rows):
        count = rows.shape[0]
        table[pl.ds(2 * first, count, stride=2), :] = rows[:, :LANES]
        table[pl.ds(2 * first + 1, count, stride=2), :] = jnp.concatenate(
            [rows[:, LANES:], jnp.zeros((count, LANES - tail), jnp.float32)], axis=1
        )

    def gather(where, buf, part=0, parts=1):
        size = targets // parts
        for k in range(GROUP):
            for target in range(part * size, (part + 1) * size):
                buf[k, 2 * target : 2 * target + 2, :] = table[pl.ds(where[k, target], 2), :]

    def both(where, into, buf, pair):
        weights = []
        for k in range(GROUP):
            operator = jnp.concatenate([far_ref[GROUP * pair + k] for far_ref in far_refs], axis=0)
            weights += [operator, jnp.zeros((surface, LANES - tail), jnp.bfloat16)]
        weights = jnp.concatenate(weights, axis=1)
        size = targets // CHUNKS
        for part in range(CHUNKS):
            rows = []
            for k in range(GROUP):
                rows += [buf[k, pl.ds(2 * part * size + half, size, stride=2), :] for half in range(2)]
            rows = jnp.concatenate([piece.astype(jnp.bfloat16) for piece in rows], axis=1)
            span = pl.ds(part * size, size)
            acc[span, :] += lax.dot_general(rows, weights, NT, preferred_element_type=jnp.float32)
            if where is not None:
                gather(where, into, part, CHUNKS)

    @pl.when(step == 0)
    def _():
        for slot in range(PHASES):
            start(slot, slot)
        acc[...] = jnp.zeros_like(acc)
        number = lax.broadcasted_iota(jnp.int32, (boxes, boxes), 1)
        for section in range(sections):
            spot = (slots_ref[:, section : section + 1] == number).astype(jnp.float32).astype(jnp.bfloat16)
            put(
                section * boxes,
                lax.dot_general(spot, blocks[section][...], NT, preferred_element_type=jnp.float32),
            )
        put(sections * boxes, coarse_ref[...].astype(jnp.bfloat16).astype(jnp.float32))
        put(sections * boxes + coarse_ref.shape[0], jnp.zeros((8, surface), jnp.float32))
        wait(0)
        gather(idx[0], buf_a)
        start(PHASES, 0)

    for pair in range(PHASES - 1):
        slot = pair + 1
        wait(slot)

        @pl.when(step <= last)
        def _():
            both(idx[slot], bufs[slot % 2], bufs[pair % 2], pair)

        start(PHASES * (step + 1) + slot, slot)

    @pl.when(step < last)
    def _():
        wait(0)

    @pl.when(step < last)
    def _():
        both(idx[0], bufs[0], bufs[1], PHASES - 1)

    @pl.when(step < last)
    def _():
        start(PHASES * (step + 2), 0)

    @pl.when(step == last)
    def _():
        both(None, None, bufs[1], PHASES - 1)
        for slot in range(PHASES):
            wait(slot)
        fine_out[...] = jnp.transpose(acc[:boxes, :])
        coarse_out[...] = acc[boxes:, :]


def translate(idx, slots, coarse, far_pieces, blocks):
    offsets, targets = idx.shape
    surface, boxes = blocks[0].shape
    sections = len(blocks)
    rows = sections * boxes + coarse.shape[0] + 8
    whole = lambda *shape: pl.BlockSpec(shape, lambda step: (0,) * len(shape))
    return pl.pallas_call(
        functools.partial(translate_kernel, sections, len(far_pieces)),
        grid=(offsets // (GROUP * PHASES),),
        in_specs=[
            pl.BlockSpec(memory_space=pl.ANY),
            whole(*slots.shape),
            whole(*coarse.shape),
        ]
        + [pl.BlockSpec((GROUP * PHASES, *piece.shape[1:]), lambda step: (step, 0, 0)) for piece in far_pieces]
        + [whole(surface, boxes) for _ in blocks],
        out_specs=[whole(surface, boxes), whole(*coarse.shape)],
        out_shape=[
            jax.ShapeDtypeStruct((surface, boxes), jnp.float32),
            jax.ShapeDtypeStruct(coarse.shape, jnp.float32),
        ],
        scratch_shapes=[
            pltpu.VMEM((2 * rows, LANES), jnp.float32),
            pltpu.VMEM((GROUP, 2 * targets, LANES), jnp.float32),
            pltpu.VMEM((GROUP, 2 * targets, LANES), jnp.float32),
            pltpu.VMEM((targets, surface), jnp.float32),
        ]
        + [pltpu.SMEM((GROUP, targets), jnp.int32) for _ in range(PHASES)]
        + [pltpu.SemaphoreType.DMA((PHASES, GROUP))],
        compiler_params=pltpu.CompilerParams(vmem_limit_bytes=51 << 20),
        name="translate",
    )(idx, slots, coarse, *far_pieces, *blocks)


def shards(fine_mult, up_operators, far_operators, far_list, ghost_list, coarse_list):
    surface, boxes = fine_mult.shape
    bits_y = lax.axis_size("hy").bit_length() - 1
    bits_x = lax.axis_size("hx").bit_length() - 1
    coarse_boxes = coarse_list.shape[1]
    bits = [("hy", bit) for bit in range(bits_y)] + [("hx", bit) for bit in range(bits_x)]
    order = bits[bits_y : bits_y + 3][::-1] + bits[bits_y + 3 :][::-1] + bits[:bits_y][::-1]
    ghosts = {bit: from_partner(fine_mult, *bit) for bit in order}
    sections = len(bits) + 1
    place = jnp.stack([lax.axis_index("hx"), lax.axis_index("hy")]).astype(jnp.int32)
    coarse = upward(place, coarse_boxes, fine_mult, up_operators)
    far_turned = jnp.transpose(far_operators, (1, 2, 0))
    strips = -(-surface // STRIP)
    cuts = [stage * strips // len(bits) for stage in range(len(bits) + 1)]
    pieces = [relayout(far_turned, low, high - low) for low, high in zip(cuts, cuts[1:])]
    stages = [bit for bit in bits if bit != order[0]] + [order[0]]
    for number, bit in enumerate(stages):
        coarse = coarse + from_partner(coarse, *bit)
        coarse, pieces[number] = lax.optimization_barrier((coarse, pieces[number]))
        if SETTLED <= number < len(stages) - 1:
            for other in order[2 * (number - SETTLED) : 2 * (number - SETTLED) + 2]:
                coarse, ghosts[other] = lax.optimization_barrier((coarse, ghosts[other]))
    blocks = [fine_mult] + [ghosts[bit] for bit in bits]
    first_coarse = sections * boxes
    zero_row = first_coarse + coarse_boxes
    idx = jnp.concatenate(
        [
            2 * jnp.where(far_list < 0, zero_row, far_list),
            2 * jnp.where(coarse_list < 0, zero_row, coarse_list + first_coarse),
        ],
        axis=1,
    )
    slots = jnp.concatenate([jnp.arange(boxes, dtype=jnp.int32)[:, None], jnp.transpose(ghost_list[0])], axis=1)
    fine_check, coarse_check = translate(idx, slots, coarse, pieces, blocks)
    return (fine_check, jnp.transpose(coarse_check))


def solution(mesh):
    placed = (
        P(None, ("hx", "hy")),
        P(),
        P(),
        P(None, ("hx", "hy")),
        P(("hx", "hy"), None, None),
        P(),
    )
    return jax.shard_map(
        shards, mesh=mesh, in_specs=placed, out_specs=(P(None, ("hx", "hy")), P()), check_vma=False
    )
```
